512 devices in a mesh: mp: 16 (over x_lo, y), dp: 32 (over z, x_hi, core).
Axes of the slice: x: 4 (x_hi: 2, x_lo: 2; x = x_hi * 2 + x_lo), y: 8, z: 8, core: 2. Of those that a mesh axis runs over, the one named last changes fastest.
Arguments:
- grad_parts: bfloat16 [32, 128, 73728], P('dp', 'mp'), may hold values from -1200 to 1200
- param: float32 [128, 73728], P('mp', 'dp'), may hold values from -40 to 40
- row_prior: float32 [128], P('mp'), may hold values from 0.05 to 1
- col_prior: float32 [73728], P('dp'), may hold values from 0.05 to 1
Outputs:
- updated: float32 [128, 73728], P('mp', 'dp')
- row_state: float32 [128], P('mp')
- col_state: float32 [73728], P('dp')
- update_rms: float32 [], replicated
The draws below stay inside these ranges and needn't reach their ends.
All inputs are finite; a program needn't handle non-finite values.
Results may differ from the reference program's by a relative error of at most 0.0003.
Values sent between devices are 32-bit elements; how exact they have to be, the bound alone decides.
No kernel may reach another device: no remote copies, remote signals or barrier semaphores. Data moves between devices by JAX's collectives and lax.ppermute only.
A program may use at most 64 MiB of HBM per device.

```python
import math
import jax
import jax.numpy as jnp
from jax import lax

COLS = 73728
ROWS = 128
REPLICAS = 32


def draw_grad_parts(key, part):
    key = jax.random.fold_in(key, 11)
    key_noise, key_owner = jax.random.split(key, 2)
    rows_index = jnp.arange(ROWS, dtype=jnp.float32)
    cols_index = jnp.arange(COLS, dtype=jnp.float32)
    noise = jnp.clip(jax.random.normal(key_noise, (REPLICAS, ROWS, COLS), jnp.float32), -5.0, 5.0)
    row_scale = jnp.exp(math.log(3.0) * rows_index / ROWS)
    col_scale = jnp.exp(math.log(3.0) * cols_index / COLS)
    owner = jax.random.permutation(key_owner, REPLICAS).astype(jnp.int32)
    block = (jnp.arange(COLS, dtype=jnp.int32) // (COLS // REPLICAS)).astype(jnp.int32)
    spike = jnp.where(block[None, :] == owner[:, None], 3.0, 1.0).astype(jnp.float32)
    values = 4.0 * noise * row_scale[None, :, None] * col_scale[None, None, :] * spike[:, None, :]
    return values.astype(jnp.bfloat16)


def draw_param(key, part):
    key = jax.random.fold_in(key, 23)
    key_noise = jax.random.fold_in(key, 0)
    rows_index = jnp.arange(ROWS, dtype=jnp.float32)
    cols_index = jnp.arange(COLS, dtype=jnp.float32)
    noise = jnp.clip(jax.random.normal(key_noise, (ROWS, COLS), jnp.float32), -5.0, 5.0)
    row_scale = jnp.exp(0.5 * math.log(10.0) * rows_index / ROWS)
    col_scale = jnp.exp(0.5 * math.log(10.0) * cols_index / COLS)
    values = 0.5 * noise * row_scale[:, None] * col_scale[None, :]
    return values.astype(jnp.float32)


def level_of(key, shape, cuts, least, high):
    def one(axis_at, blocks):
        heights = jax.random.uniform(jax.random.fold_in(jax.random.fold_in(key, 6), axis_at), (blocks,), jnp.float32, least / len(cuts), high / len(cuts))
        return jnp.repeat(jnp.exp(heights), shape[axis_at] // blocks).reshape((-1,) + (1,) * (len(shape) - axis_at - 1))

    loudness = one(*cuts[0])
    for cut in cuts[1:]:
        loudness = loudness * one(*cut)
    return loudness


def setup_inputs(seed: int = 0) -> dict:
    key_list = jax.random.split(jax.random.key(seed), 5)
    return {
        "grad_parts": draw_grad_parts(jax.random.fold_in(key_list[4], 71), 0),
        "param": draw_param(jax.random.fold_in(key_list[4], 71), 0),
        "row_prior": jnp.clip(jnp.exp(math.log(1.0) - 2.9957323 * jax.random.uniform(key_list[2], (ROWS,), jnp.float32) ** level_of(key_list[2], (ROWS,), ((0, 16),), -0.2, 0.2)), 0.05, 1.0),
        "col_prior": jnp.clip(jnp.exp(math.log(1.0) - 2.9957323 * jax.random.uniform(key_list[3], (COLS,), jnp.float32) ** level_of(key_list[3], (COLS,), ((0, 32),), -0.2, 0.2)), 0.05, 1.0),
    }


def reference(grad_parts, param, row_prior, col_prior):

    def accumulate(index, total):
        piece = lax.dynamic_index_in_dim(grad_parts, index, 0, keepdims=False)
        return total + piece.astype(jnp.float32)
    summed = lax.fori_loop(0, REPLICAS, accumulate, jnp.zeros((ROWS, COLS), jnp.float32))
    gradient = summed / REPLICAS
    squares = gradient * gradient + 1e-30
    row_state = 0.9 * row_prior + 0.1 * lax.optimization_barrier(jnp.sum(squares, axis=1)) / COLS
    col_state = 0.9 * col_prior + 0.1 * lax.optimization_barrier(jnp.sum(squares, axis=0)) / ROWS
    row_total = jnp.sum(row_state) / ROWS
    update = gradient / jnp.sqrt(row_state[:, None] * col_state[None, :] / row_total)
    entries = ROWS * COLS
    update_rms = jnp.sqrt(jnp.sum(update * update) / entries)
    param_rms = jnp.sqrt(jnp.sum(param * param) / entries + 1e-06)
    updated = param - 0.01 * param_rms * update / jnp.maximum(1.0, update_rms)
    return (updated, row_state, col_state, update_rms)
```

```python
import jax
import jax.numpy as jnp
from jax import lax
from jax.sharding import PartitionSpec as P

COLS = 73728


def everyone(value, axis, size):
    width = value.shape[0]
    sent = jnp.broadcast_to(value[None, None, :], (size, 1, width))
    return lax.all_to_all(sent, axis, 0, 0, tiled=True)


def on_device(grad_parts, param, row_prior, col_prior):
    replicas = lax.axis_size("dp")
    slabs = lax.axis_size("mp")
    rows = grad_parts.shape[1]
    own = param.shape[1]
    all_rows = rows * slabs
    pairs = replicas // 2
    core = lax.axis_index("dp") % 2

    blocks = grad_parts[0].reshape(rows, pairs, 2, own).transpose(2, 1, 0, 3)
    sent = lax.dynamic_index_in_dim(blocks, 1 - core, 0, keepdims=False).astype(jnp.float32)
    kept = lax.dynamic_index_in_dim(blocks, core, 0, keepdims=False)
    got = lax.ppermute(sent, "dp", [(i, i ^ 1) for i in range(replicas)])
    both = kept.astype(jnp.float32) + got
    same_core = [[2 * i + c for i in range(pairs)] for c in range(2)]
    parts = lax.all_to_all(both, "dp", 0, 0, tiled=True, axis_index_groups=same_core)
    gradient = jnp.sum(parts, axis=0) / replicas

    power = gradient * gradient
    squares = power + 1e-30
    col_sum = jnp.sum(everyone(jnp.sum(squares, axis=0), "mp", slabs), axis=(0, 1))
    col_state = 0.9 * col_prior + 0.1 * col_sum / all_rows

    row_part = jnp.concatenate(
        [
            jnp.sum(squares, axis=1),
            jnp.sum(power / col_state[None, :], axis=1),
            jnp.sum(param * param, axis=1),
        ]
    )
    row_part = jnp.pad(row_part, (0, 128 - 3 * rows))
    row_all = jnp.sum(everyone(row_part, "dp", replicas), axis=(0, 1))
    row_sum, scaled_sum, param_rows = (row_all[i * rows : (i + 1) * rows] for i in range(3))
    row_state = 0.9 * row_prior + 0.1 * row_sum / COLS

    last = jnp.stack([jnp.sum(row_state), jnp.sum(scaled_sum / row_state), jnp.sum(param_rows)])
    last_all = jnp.sum(everyone(jnp.pad(last, (0, 125)), "mp", slabs), axis=(0, 1))
    row_total = last_all[0] / all_rows
    entries = float(all_rows * COLS)
    update_rms = jnp.sqrt(row_total * last_all[1] / entries)
    param_rms = jnp.sqrt(last_all[2] / entries + 1e-06)
    update = gradient / jnp.sqrt(row_state[:, None] * col_state[None, :] / row_total)
    updated = param - 0.01 * param_rms * update / jnp.maximum(1.0, update_rms)
    return (updated, row_state, col_state, update_rms)


def solution(mesh):
    in_specs = (P("dp", "mp", None), P("mp", "dp"), P("mp"), P("dp"))
    out_specs = (P("mp", "dp"), P("mp"), P("dp"), P())
    return jax.shard_map(
        on_device, mesh=mesh, in_specs=in_specs, out_specs=out_specs, check_vma=False
    )
```

```python
import jax
import jax.numpy as jnp
from jax import lax
from jax.sharding import PartitionSpec as P

COLS = 73728


def everyone(value, axis, size):
    sent = jnp.broadcast_to(value[None], (size, *value.shape))
    return lax.all_to_all(sent, axis, 0, 0, tiled=True)


def on_device(grad_parts, param, row_prior, col_prior):
    replicas = lax.axis_size("dp")
    slabs = lax.axis_size("mp")
    rows = grad_parts.shape[1]
    own = param.shape[1]
    all_rows = rows * slabs
    pairs = replicas // 2
    core = lax.axis_index("dp") % 2

    blocks = grad_parts[0].reshape(rows, pairs, 2, own).transpose(2, 1, 0, 3)
    sent = lax.dynamic_index_in_dim(blocks, 1 - core, 0, keepdims=False).astype(jnp.float32)
    kept = lax.dynamic_index_in_dim(blocks, core, 0, keepdims=False)
    got = lax.ppermute(sent, "dp", [(i, i ^ 1) for i in range(replicas)])
    kept, param_part = lax.optimization_barrier((kept, jnp.sum(param * param, axis=1)))
    both = kept.astype(jnp.float32) + got
    far = replicas // 8
    both = jnp.concatenate([both[4 * f + n][None] for n in range(4) for f in range(far)])
    both = both.reshape(4, far, rows, own)
    near_groups = [[8 * f + 2 * n + c for n in range(4)] for f in range(far) for c in range(2)]
    parts = lax.all_to_all(both, "dp", 0, 0, tiled=True, axis_index_groups=near_groups)
    far_groups = [[8 * f + 2 * n + c for f in range(far)] for n in range(4) for c in range(2)]
    parts = jnp.sum(parts, axis=0)
    parts = lax.all_to_all(parts, "dp", 0, 0, tiled=True, axis_index_groups=far_groups)
    gradient = jnp.sum(parts, axis=0) / replicas

    power = gradient * gradient
    squares = power + 1e-30
    col_sum = jnp.sum(everyone(jnp.sum(squares, axis=0)[None], "mp", slabs), axis=(0, 1))
    col_state = 0.9 * col_prior + 0.1 * col_sum / all_rows

    row_part = jnp.stack(
        [jnp.sum(squares, axis=1), jnp.sum(power / col_state[None, :], axis=1), param_part]
    )
    row_all = jnp.sum(everyone(row_part, "dp", replicas), axis=0)
    row_state = 0.9 * row_prior + 0.1 * row_all[0] / COLS
    last = jnp.sum(jnp.stack([row_state, row_all[1] / row_state, row_all[2]]), axis=1)
    update = gradient / jnp.sqrt(row_state[:, None] * col_state[None, :])
    last, update = lax.optimization_barrier((last, update))
    last_all = jnp.sum(everyone(jnp.broadcast_to(last[:, None], (3, rows)), "mp", slabs), axis=0)
    row_total = last_all[0] / all_rows
    entries = float(all_rows * COLS)
    update_rms = jnp.sqrt(row_total * last_all[1] / entries)
    param_rms = jnp.sqrt(last_all[2] / entries + 1e-06)
    scale = 0.01 * param_rms * jnp.sqrt(row_total) / jnp.maximum(1.0, update_rms)
    updated = param - scale[:, None] * update
    return (updated, row_state, col_state, update_rms[0])


def solution(mesh):
    in_specs = (P("dp", "mp", None), P("mp", "dp"), P("mp"), P("dp"))
    out_specs = (P("mp", "dp"), P("mp"), P("dp"), P())
    return jax.shard_map(
        on_device, mesh=mesh, in_specs=in_specs, out_specs=out_specs, check_vma=False
    )
```

```python
import jax
import jax.numpy as jnp
from jax import lax
from jax.sharding import PartitionSpec as P

COLS = 73728


def everyone(value, axis, size):
    sent = jnp.broadcast_to(value[None], (size, *value.shape))
    return lax.all_to_all(sent, axis, 0, 0, tiled=True)


def on_device(grad_parts, param, row_prior, col_prior):
    replicas = lax.axis_size("dp")
    slabs = lax.axis_size("mp")
    rows = grad_parts.shape[1]
    own = param.shape[1]
    all_rows = rows * slabs
    pairs = replicas // 2
    core = lax.axis_index("dp") % 2

    blocks = grad_parts[0].reshape(rows, pairs, 2, own).transpose(2, 1, 0, 3)
    sent = lax.dynamic_index_in_dim(blocks, 1 - core, 0, keepdims=False).astype(jnp.float32)
    kept = lax.dynamic_index_in_dim(blocks, core, 0, keepdims=False)
    got = lax.ppermute(sent, "dp", [(i, i ^ 1) for i in range(replicas)])
    lanes = 128
    wide = slabs * lanes
    rest = (own - wide) // slabs
    slab = lax.axis_index("mp")
    first_row = (slab * rows).astype(jnp.uint32)
    old_part = lax.optimization_barrier(0.9 * col_prior)
    tile_old = lax.dynamic_slice(old_part, ((slab * lanes).astype(jnp.uint32),), (lanes,))
    rest_old = lax.dynamic_slice(old_part, ((wide + slab * rest).astype(jnp.uint32),), (rest,))
    own_rows = jnp.arange(all_rows) // rows == slab
    priors = jnp.where(own_rows, jnp.tile(row_prior, slabs), 0.0)
    param_part = jnp.sum(param * param, axis=1)
    got, param_part, priors, tile_old, rest_old, first_row = lax.optimization_barrier(
        (got, param_part, priors, tile_old, rest_old, first_row)
    )
    both = kept.astype(jnp.float32) + got
    far = replicas // 8
    both = jnp.concatenate([both[4 * f + n][None] for n in range(4) for f in range(far)])
    both = both.reshape(4, far, rows, own)
    near_groups = [[8 * f + 2 * n + c for n in range(4)] for f in range(far) for c in range(2)]
    parts = lax.all_to_all(both, "dp", 0, 0, tiled=True, axis_index_groups=near_groups)
    parts = jnp.sum(parts, axis=0)

    piece = rows * (lanes + rest)
    main = parts[:, :, :wide].reshape(far, rows, slabs, lanes).transpose(0, 2, 1, 3)
    side = parts[:, :, wide:].reshape(far, rows, slabs, rest).transpose(0, 2, 1, 3)
    sent = jnp.concatenate(
        [main.reshape(far * slabs, 1, rows * lanes), side.reshape(far * slabs, 1, rows * rest)],
        axis=2,
    )
    all_groups = [
        [m * replicas + 8 * f + 2 * n + c for f in range(far) for m in range(slabs)]
        for n in range(4)
        for c in range(2)
    ]
    parts = lax.all_to_all(sent, ("mp", "dp"), 0, 0, tiled=True, axis_index_groups=all_groups)
    gradient = jnp.sum(parts.reshape(far, slabs, 1, piece), axis=0) / replicas

    power = gradient * gradient
    squares = power + 1e-30
    cut = rows * lanes

    def halves(value):
        value = value[:, 0]
        return value[:, :cut].reshape(slabs, rows, lanes), value[:, cut:].reshape(slabs, rows, rest)

    cols = [
        old + 0.1 * jnp.sum(value, axis=(0, 1)) / all_rows
        for old, value in zip((tile_old, rest_old), halves(squares))
    ]

    def along_rows(tile_value, rest_value):
        gap = lanes - rest
        return jnp.sum(tile_value + jnp.pad(rest_value, ((0, 0), (0, 0), (0, gap))), axis=2)

    row_part = along_rows(*halves(squares))
    scaled_part = along_rows(*(value / c for value, c in zip(halves(power), cols)))
    sums = jnp.concatenate(
        [
            jnp.stack([row_part, scaled_part]).reshape(2 * all_rows),
            jnp.pad(param_part, (0, all_rows - rows)),
        ]
    )[None]
    known = jnp.concatenate([jnp.pad(jnp.concatenate(cols), (0, 2 * lanes - lanes - rest)), priors])
    known = jnp.broadcast_to(known, (slabs, 1, 2 * lanes + all_rows))
    known = jnp.concatenate([gradient, known], axis=2)
    sums, known = lax.optimization_barrier((sums, known))
    sums = jnp.sum(everyone(sums, "dp", replicas), axis=0)

    known = jnp.concatenate([known, jnp.broadcast_to(sums, (slabs, *sums.shape))], axis=2)
    known = lax.all_to_all(known, "mp", 0, 0, tiled=True)
    at = piece + 2 * lanes
    priors = jnp.sum(known[:, 0, at : at + all_rows], axis=0)
    sums = jnp.sum(known[:, 0, at + all_rows :], axis=0)
    row_sum, scaled_sum, param_sum = (sums[i * all_rows : (i + 1) * all_rows] for i in range(3))
    row_states = 0.9 * priors + 0.1 * row_sum / COLS
    totals = jnp.stack([row_states, scaled_sum / row_states, param_sum])
    totals = lax.optimization_barrier(jnp.broadcast_to(totals[:, None, :], (3, rows, all_rows)))
    totals = jnp.sum(totals, axis=2)
    row_state = lax.dynamic_slice(row_states, (first_row,), (rows,))
    main, side = halves(known[:, :, :piece])
    gradient = jnp.concatenate(
        [
            main.transpose(1, 0, 2).reshape(rows, wide),
            side.transpose(1, 0, 2).reshape(rows, own - wide),
        ],
        axis=1,
    )
    col_state = jnp.concatenate(
        [
            known[:, 0, piece : piece + lanes].reshape(wide),
            known[:, 0, piece + lanes : piece + lanes + rest].reshape(own - wide),
        ]
    )
    row_total = totals[0] / all_rows
    entries = float(all_rows * COLS)
    update_rms = jnp.sqrt(row_total * totals[1] / entries)
    param_rms = jnp.sqrt(totals[2] / entries + 1e-06)
    scale = 0.01 * param_rms * jnp.sqrt(row_total) / jnp.maximum(1.0, update_rms)
    update = gradient / jnp.sqrt(row_state[:, None] * col_state[None, :])
    updated = param - scale[:, None] * update
    return (updated, row_state, col_state, update_rms[0])


def solution(mesh):
    in_specs = (P("dp", "mp", None), P("mp", "dp"), P("mp"), P("dp"))
    out_specs = (P("mp", "dp"), P("mp"), P("dp"), P())
    return jax.shard_map(
        on_device, mesh=mesh, in_specs=in_specs, out_specs=out_specs, check_vma=False
    )
```

```python
import jax
import jax.numpy as jnp
from jax import lax
from jax.sharding import PartitionSpec as P

COLS = 73728
LANES = 128


def everyone(value, axis, size):
    sent = jnp.broadcast_to(value[None], (size, *value.shape))
    return lax.all_to_all(sent, axis, 0, 0, tiled=True)


def on_device(grad_parts, param, row_prior, col_prior):
    replicas = lax.axis_size("dp")
    slabs = lax.axis_size("mp")
    rows = grad_parts.shape[1]
    own = param.shape[1]
    all_rows = rows * slabs
    pairs = replicas // 2
    core = lax.axis_index("dp") % 2
    far, near, wide = replicas // 8, 4, 2
    deep = slabs // wide
    half = own // wide
    tiles = deep * LANES
    rest = (half - tiles) // deep
    slab = lax.axis_index("mp")
    across, along = slab // deep, slab % deep

    def device(f, n, c, x, y):
        return (deep * x + y) * replicas + 8 * f + 2 * n + c

    blocks = grad_parts[0].reshape(rows, pairs, 2, own).transpose(2, 1, 0, 3)
    sent = lax.dynamic_index_in_dim(blocks, 1 - core, 0, keepdims=False).astype(jnp.float32)
    kept = lax.dynamic_index_in_dim(blocks, core, 0, keepdims=False)
    got = lax.ppermute(sent, "dp", [(i, i ^ 1) for i in range(replicas)])
    place = wide * along + across
    first_row = (place * rows).astype(jnp.uint32)
    old_part = lax.optimization_barrier(0.9 * col_prior)
    tile_at = half * across + LANES * along
    rest_at = half * across + tiles + rest * along
    tile_old = lax.dynamic_slice(old_part, (tile_at.astype(jnp.uint32),), (LANES,))
    rest_old = lax.dynamic_slice(old_part, (rest_at.astype(jnp.uint32),), (rest,))
    priors = jnp.where(jnp.arange(all_rows) // rows == place, jnp.tile(row_prior, slabs), 0.0)
    param_part = jnp.sum(param * param, axis=1)
    got, param_part, priors, tile_old, rest_old, first_row = lax.optimization_barrier(
        (got, param_part, priors, tile_old, rest_old, first_row)
    )
    both = kept.astype(jnp.float32) + got

    both = jnp.concatenate(
        [
            both[near * f + n, :, half * x : half * (x + 1)][None]
            for n in range(near)
            for x in range(wide)
            for f in range(far)
        ]
    ).reshape(near * wide, far, rows, half)
    near_groups = [
        [device(f, n, c, x, y) for n in range(near) for x in range(wide)]
        for f in range(far)
        for c in range(2)
        for y in range(deep)
    ]
    parts = lax.all_to_all(both, ("mp", "dp"), 0, 0, tiled=True, axis_index_groups=near_groups)
    parts = jnp.sum(parts.reshape(near, wide, far, rows, half), axis=0)

    main = parts[..., :tiles].reshape(wide, far, rows, deep, LANES).transpose(1, 3, 0, 2, 4)
    side = parts[..., tiles:].reshape(wide, far, rows, deep, rest).transpose(1, 3, 0, 2, 4)
    cut = rows * LANES
    piece = cut + rows * rest
    sent = jnp.concatenate(
        [
            main.reshape(far * deep, 1, wide * cut),
            side.reshape(far * deep, 1, wide * rows * rest),
        ],
        axis=2,
    )
    far_groups = [
        [device(f, n, c, x, y) for f in range(far) for y in range(deep)]
        for n in range(near)
        for c in range(2)
        for x in range(wide)
    ]
    parts = lax.all_to_all(sent, ("mp", "dp"), 0, 0, tiled=True, axis_index_groups=far_groups)
    gradient = jnp.sum(parts.reshape(far, deep, 1, wide * piece), axis=0) / replicas

    flat = gradient[:, 0]
    halves = (
        flat[:, : wide * cut].reshape(slabs, rows, LANES),
        flat[:, wide * cut :].reshape(slabs, rows, rest),
    )
    power = [value * value for value in halves]
    squares = [value + 1e-30 for value in power]
    cols = [
        old + 0.1 * jnp.sum(value, axis=(0, 1)) / all_rows
        for old, value in zip((tile_old, rest_old), squares)
    ]

    def along_rows(tile_value, rest_value):
        gap = LANES - rest
        return jnp.sum(tile_value + jnp.pad(rest_value, ((0, 0), (0, 0), (0, gap))), axis=2)

    row_part = along_rows(*squares)
    scaled_part = along_rows(*(value / c for value, c in zip(power, cols)))
    sums = jnp.concatenate(
        [
            jnp.stack([row_part, scaled_part]).reshape(2 * all_rows),
            jnp.pad(param_part, (0, all_rows - rows)),
        ]
    )[None]
    known = jnp.concatenate([jnp.pad(jnp.concatenate(cols), (0, LANES - rest)), priors])
    known = jnp.broadcast_to(known, (slabs, 1, 2 * LANES + all_rows))
    main = gradient[:, 0, : wide * cut].reshape(deep, wide, cut).transpose(1, 0, 2)
    side = gradient[:, 0, wide * cut :].reshape(deep, wide, piece - cut).transpose(1, 0, 2)
    known = jnp.concatenate(
        [main.reshape(slabs, 1, cut), side.reshape(slabs, 1, piece - cut), known], axis=2
    )
    sums, known = lax.optimization_barrier((sums, known))
    sums = jnp.sum(everyone(sums, "dp", replicas), axis=0)

    known = jnp.concatenate([known, jnp.broadcast_to(sums, (slabs, *sums.shape))], axis=2)
    known = lax.all_to_all(known, "mp", 0, 0, tiled=True)
    at = piece + 2 * LANES
    priors = jnp.sum(known[:, 0, at : at + all_rows], axis=0)
    sums = jnp.sum(known[:, 0, at + all_rows :], axis=0)
    row_sum, scaled_sum, param_sum = (sums[i * all_rows : (i + 1) * all_rows] for i in range(3))
    row_states = 0.9 * priors + 0.1 * row_sum / COLS
    totals = jnp.stack([row_states, scaled_sum / row_states, param_sum])
    totals = lax.optimization_barrier(jnp.broadcast_to(totals[:, None, :], (3, rows, all_rows)))
    totals = jnp.sum(totals, axis=2)
    row_state = lax.dynamic_slice(row_states, (first_row,), (rows,))

    def in_columns(start, width, lines):
        value = known[:, 0, start : start + lines * width].reshape(slabs, lines, width)
        value = value.transpose(1, 0, 2).reshape(lines, wide, deep * width)
        return [value[:, x] for x in range(wide)]

    def whole(start, lines):
        tile_value = in_columns(start, LANES, lines)
        rest_value = in_columns(start + lines * LANES, rest, lines)
        return jnp.concatenate(
            [v for pair in zip(tile_value, rest_value) for v in pair], axis=1
        )

    gradient = whole(0, rows)
    col_state = whole(piece, 1)[0]
    row_total = totals[0] / all_rows
    entries = float(all_rows * COLS)
    update_rms = jnp.sqrt(row_total * totals[1] / entries)
    param_rms = jnp.sqrt(totals[2] / entries + 1e-06)
    scale = 0.01 * param_rms * jnp.sqrt(row_total) / jnp.maximum(1.0, update_rms)
    update = gradient / jnp.sqrt(row_state[:, None] * col_state[None, :])
    updated = param - scale[:, None] * update
    return (updated, row_state, col_state, update_rms[0])


def solution(mesh):
    in_specs = (P("dp", "mp", None), P("mp", "dp"), P("mp"), P("dp"))
    out_specs = (P("mp", "dp"), P("mp"), P("dp"), P())
    return jax.shard_map(
        on_device, mesh=mesh, in_specs=in_specs, out_specs=out_specs, check_vma=False
    )
```

```python
import jax
import jax.numpy as jnp
from jax import lax
from jax.sharding import PartitionSpec as P

COLS = 73728
LANES = 128


def everyone(value, axis, size):
    sent = jnp.broadcast_to(value[None], (size, *value.shape))
    return lax.all_to_all(sent, axis, 0, 0, tiled=True)


def on_device(grad_parts, param, row_prior, col_prior):
    replicas = lax.axis_size("dp")
    slabs = lax.axis_size("mp")
    rows = grad_parts.shape[1]
    own = param.shape[1]
    all_rows = rows * slabs
    pairs = replicas // 2
    core = lax.axis_index("dp") % 2
    far, near, wide = replicas // 8, 4, 2
    deep = slabs // wide
    half = own // wide
    tiles = deep * LANES
    rest = (half - tiles) // deep
    slab = lax.axis_index("mp")
    across, along = slab // deep, slab % deep

    def device(f, n, c, x, y):
        return (deep * x + y) * replicas + 8 * f + 2 * n + c

    blocks = grad_parts[0].reshape(rows, pairs, 2, own).transpose(2, 1, 0, 3)
    sent = lax.dynamic_index_in_dim(blocks, 1 - core, 0, keepdims=False).astype(jnp.float32)
    kept = lax.dynamic_index_in_dim(blocks, core, 0, keepdims=False)
    got = lax.ppermute(sent, "dp", [(i, i ^ 1) for i in range(replicas)])
    place = wide * along + across
    first_row = (place * rows).astype(jnp.uint32)
    old_part = lax.optimization_barrier(0.9 * col_prior)
    tile_at = half * across + LANES * along
    rest_at = half * across + tiles + rest * along
    tile_old = lax.dynamic_slice(old_part, (tile_at.astype(jnp.uint32),), (LANES,))
    rest_old = lax.dynamic_slice(old_part, (rest_at.astype(jnp.uint32),), (rest,))
    own_slab = jnp.arange(slabs)[:, None] == place
    old_rows = jnp.where(own_slab, (0.9 * row_prior / replicas)[None, :], 0.0)
    param_part = jnp.sum(param * param, axis=1)
    got, param_part, old_rows, tile_old, rest_old, first_row = lax.optimization_barrier(
        (got, param_part, old_rows, tile_old, rest_old, first_row)
    )
    both = kept.astype(jnp.float32) + got

    both = both.reshape(far, near, rows, own)
    both = jnp.concatenate(
        [both[:, n, :, half * x : half * (x + 1)] for n in range(near) for x in range(wide)]
    ).reshape(near * wide, far, rows, half)
    near_groups = [
        [device(f, n, c, x, y) for n in range(near) for x in range(wide)]
        for f in range(far)
        for c in range(2)
        for y in range(deep)
    ]
    parts = lax.all_to_all(both, ("mp", "dp"), 0, 0, tiled=True, axis_index_groups=near_groups)
    parts = jnp.sum(parts.reshape(near, wide, far, rows, half), axis=0)

    main = parts[..., :tiles].reshape(wide, far, rows, deep, LANES).transpose(1, 3, 0, 2, 4)
    side = parts[..., tiles:].reshape(wide, far, rows, deep, rest).transpose(1, 3, 0, 2, 4)
    cut = rows * LANES
    piece = cut + rows * rest
    sent = jnp.concatenate(
        [
            main.reshape(far * deep, 1, wide * cut),
            side.reshape(far * deep, 1, wide * rows * rest),
        ],
        axis=2,
    )
    far_groups = [
        [device(f, n, c, x, y) for f in range(far) for y in range(deep)]
        for n in range(near)
        for c in range(2)
        for x in range(wide)
    ]
    parts = lax.all_to_all(sent, ("mp", "dp"), 0, 0, tiled=True, axis_index_groups=far_groups)
    gradient = jnp.sum(parts.reshape(far, deep, 1, wide * piece), axis=0) / replicas

    flat = gradient[:, 0]
    halves = (
        flat[:, : wide * cut].reshape(slabs, rows, LANES),
        flat[:, wide * cut :].reshape(slabs, rows, rest),
    )
    power = [value * value for value in halves]
    squares = [value + 1e-30 for value in power]
    cols = [
        old + 0.1 * jnp.sum(value, axis=(0, 1)) / all_rows
        for old, value in zip((tile_old, rest_old), squares)
    ]

    def along_rows(tile_value, rest_value):
        gap = LANES - rest
        return jnp.sum(tile_value + jnp.pad(rest_value, ((0, 0), (0, 0), (0, gap))), axis=2)

    row_part = old_rows + 0.1 * along_rows(*squares) / COLS
    scaled_part = along_rows(*(value / c for value, c in zip(power, cols)))
    sums = jnp.concatenate(
        [
            jnp.stack([row_part, scaled_part]).reshape(2 * all_rows),
            jnp.pad(param_part, (0, all_rows - rows)),
        ]
    )[None]
    gap = 2 * rows
    rest_cols = jnp.pad(cols[1], (2 * all_rows + gap, all_rows - gap - rest))[None]
    known = jnp.broadcast_to(cols[0], (slabs, 1, LANES))
    main = gradient[:, 0, : wide * cut].reshape(deep, wide, cut).transpose(1, 0, 2)
    side = gradient[:, 0, wide * cut :].reshape(deep, wide, piece - cut).transpose(1, 0, 2)
    known = jnp.concatenate(
        [main.reshape(slabs, 1, cut), side.reshape(slabs, 1, piece - cut), known], axis=2
    )
    sums, known, rest_cols = lax.optimization_barrier((sums, known, rest_cols))
    sums = jnp.sum(everyone(sums, "dp", replicas), axis=0) + rest_cols

    known = jnp.concatenate([known, jnp.broadcast_to(sums, (slabs, *sums.shape))], axis=2)
    known = lax.all_to_all(known, "mp", 0, 0, tiled=True)
    at = piece + LANES
    sums = jnp.sum(known[:, 0, at:], axis=0)
    row_states, scaled_sum, param_sum = (sums[i * all_rows : (i + 1) * all_rows] for i in range(3))
    param_sum = jnp.where(jnp.arange(all_rows) < rows, param_sum, 0.0)
    totals = jnp.stack([row_states, scaled_sum / row_states, param_sum])
    totals = lax.optimization_barrier(jnp.broadcast_to(totals[:, None, :], (3, rows, all_rows)))
    totals = jnp.sum(totals, axis=2)
    row_state = lax.dynamic_slice(row_states, (first_row,), (rows,))

    def in_columns(start, width, lines):
        value = known[:, 0, start : start + lines * width].reshape(slabs, lines, width)
        value = value.transpose(1, 0, 2).reshape(lines, wide, deep * width)
        return [value[:, x] for x in range(wide)]

    def whole(tile_start, rest_start, lines):
        tile_value = in_columns(tile_start, LANES, lines)
        rest_value = in_columns(rest_start, rest, lines)
        return jnp.concatenate(
            [v for pair in zip(tile_value, rest_value) for v in pair], axis=1
        )

    gradient = whole(0, cut, rows)
    col_state = whole(piece, at + 2 * all_rows + gap, 1)[0]
    row_total = totals[0] / all_rows
    entries = float(all_rows * COLS)
    update_rms = jnp.sqrt(row_total * totals[1] / entries)
    param_rms = jnp.sqrt(totals[2] / entries + 1e-06)
    scale = 0.01 * param_rms * jnp.sqrt(row_total) / jnp.maximum(1.0, update_rms)
    update = gradient / jnp.sqrt(row_state[:, None] * col_state[None, :])
    updated = param - scale[:, None] * update
    return (updated, row_state, col_state, update_rms[0])


def solution(mesh):
    in_specs = (P("dp", "mp", None), P("mp", "dp"), P("mp"), P("dp"))
    out_specs = (P("mp", "dp"), P("mp"), P("dp"), P())
    return jax.shard_map(
        on_device, mesh=mesh, in_specs=in_specs, out_specs=out_specs, check_vma=False
    )
```

```python
import jax
import jax.numpy as jnp
from jax import lax
from jax.sharding import PartitionSpec as P

COLS = 73728
LANES = 128


def everyone(value, axis, size):
    sent = jnp.broadcast_to(value[None], (size, *value.shape))
    return lax.all_to_all(sent, axis, 0, 0, tiled=True)


def on_device(grad_parts, param, row_prior, col_prior):
    replicas = lax.axis_size("dp")
    slabs = lax.axis_size("mp")
    rows = grad_parts.shape[1]
    own = param.shape[1]
    all_rows = rows * slabs
    pairs = replicas // 2
    core = lax.axis_index("dp") % 2
    far, near, wide = replicas // 8, 4, 2
    deep = slabs // wide
    half = own // wide
    tiles = deep * LANES
    rest = (half - tiles) // deep
    slab = lax.axis_index("mp")
    across, along = slab // deep, slab % deep

    def device(f, n, c, x, y):
        return (deep * x + y) * replicas + 8 * f + 2 * n + c

    blocks = grad_parts[0].reshape(rows, pairs, 2, own).transpose(2, 1, 0, 3)
    sent = lax.dynamic_index_in_dim(blocks, 1 - core, 0, keepdims=False).astype(jnp.float32)
    kept = lax.dynamic_index_in_dim(blocks, core, 0, keepdims=False)
    got = lax.ppermute(sent, "dp", [(i, i ^ 1) for i in range(replicas)])
    place = wide * along + across
    first_row = (place * rows).astype(jnp.uint32)
    old_part = lax.optimization_barrier(0.9 * col_prior)
    tile_at = half * across + LANES * along
    rest_at = half * across + tiles + rest * along
    tile_old = lax.dynamic_slice(old_part, (tile_at.astype(jnp.uint32),), (LANES,))
    rest_old = lax.dynamic_slice(old_part, (rest_at.astype(jnp.uint32),), (rest,))
    own_slab = jnp.arange(slabs)[:, None] == place
    old_rows = jnp.where(own_slab, (0.9 * row_prior / replicas)[None, :], 0.0)
    param_part = jnp.sum(param * param, axis=1)
    got, param_part, old_rows, tile_old, rest_old, first_row = lax.optimization_barrier(
        (got, param_part, old_rows, tile_old, rest_old, first_row)
    )
    both = kept.astype(jnp.float32) + got

    both = both.reshape(far, near, rows, own)
    both = jnp.concatenate(
        [both[:, n, :, half * x : half * (x + 1)] for n in range(near) for x in range(wide)]
    ).reshape(near * wide, far, rows, half)
    near_groups = [
        [device(f, n, c, x, y) for n in range(near) for x in range(wide)]
        for f in range(far)
        for c in range(2)
        for y in range(deep)
    ]
    parts = lax.all_to_all(both, ("mp", "dp"), 0, 0, tiled=True, axis_index_groups=near_groups)
    parts = jnp.sum(parts.reshape(near, wide, far, rows, half), axis=0)

    main = parts[..., :tiles].reshape(wide, far, rows, deep, LANES).transpose(1, 3, 0, 2, 4)
    side = parts[..., tiles:].reshape(wide, far, rows, deep, rest).transpose(1, 3, 0, 2, 4)
    cut = rows * LANES
    piece = cut + rows * rest
    sent = jnp.concatenate(
        [
            main.reshape(far * deep, 1, wide * cut),
            side.reshape(far * deep, 1, wide * rows * rest),
        ],
        axis=2,
    )
    far_groups = [
        [device(f, n, c, x, y) for f in range(far) for y in range(deep)]
        for n in range(near)
        for c in range(2)
        for x in range(wide)
    ]
    parts = lax.all_to_all(sent, ("mp", "dp"), 0, 0, tiled=True, axis_index_groups=far_groups)
    gradient = jnp.sum(parts.reshape(far, deep, 1, wide * piece), axis=0) / replicas

    flat = gradient[:, 0]
    halves = (
        flat[:, : wide * cut].reshape(slabs, rows, LANES),
        flat[:, wide * cut :].reshape(slabs, rows, rest),
    )
    power = [value * value for value in halves]
    squares = [value + 1e-30 for value in power]
    cols = [
        old + 0.1 * jnp.sum(value, axis=(0, 1)) / all_rows
        for old, value in zip((tile_old, rest_old), squares)
    ]

    def along_rows(tile_value, rest_value):
        gap = LANES - rest
        return jnp.sum(tile_value + jnp.pad(rest_value, ((0, 0), (0, 0), (0, gap))), axis=2)

    row_part = old_rows + 0.1 * along_rows(*squares) / COLS
    scaled_part = along_rows(*(value / c for value, c in zip(power, cols)))
    sums = jnp.concatenate(
        [
            jnp.stack([row_part, scaled_part]).reshape(2 * all_rows),
            jnp.pad(param_part, (0, all_rows - rows)),
        ]
    )[None]
    gap = 2 * rows
    rest_cols = jnp.pad(cols[1], (2 * all_rows + gap, all_rows - gap - rest))[None]
    known = jnp.broadcast_to(cols[0], (slabs, 1, LANES))
    main = gradient[:, 0, : wide * cut].reshape(deep, wide, cut).transpose(1, 0, 2)
    side = gradient[:, 0, wide * cut :].reshape(deep, wide, piece - cut).transpose(1, 0, 2)
    known = jnp.concatenate(
        [main.reshape(slabs, 1, cut), side.reshape(slabs, 1, piece - cut), known], axis=2
    )
    sums, known, rest_cols = lax.optimization_barrier((sums, known, rest_cols))
    sums = jnp.sum(everyone(sums, "dp", replicas), axis=0) + rest_cols

    known = jnp.concatenate([known, jnp.broadcast_to(sums, (slabs, *sums.shape))], axis=2)
    known = lax.all_to_all(known, "mp", 0, 0, tiled=True)
    at = piece + LANES
    sums = jnp.sum(known[:, 0, at:], axis=0)
    row_states, scaled_sum, param_sum = (sums[i * all_rows : (i + 1) * all_rows] for i in range(3))
    param_sum = jnp.where(jnp.arange(all_rows) < rows, param_sum, 0.0)
    totals = jnp.stack([row_states, scaled_sum / row_states, param_sum])
    totals = lax.optimization_barrier(jnp.broadcast_to(totals[:, None, :], (3, rows, all_rows)))
    totals = jnp.sum(totals, axis=2)
    row_state = lax.dynamic_slice(row_states, (first_row,), (rows,))

    def in_columns(start, width, lines):
        value = known[:, 0, start : start + lines * width].reshape(slabs, lines, width)
        value = value.transpose(1, 0, 2).reshape(lines, wide, deep * width)
        return [value[:, x] for x in range(wide)]

    def whole(tile_start, rest_start, lines):
        tile_value = in_columns(tile_start, LANES, lines)
        rest_value = in_columns(rest_start, rest, lines)
        return jnp.concatenate(
            [v for pair in zip(tile_value, rest_value) for v in pair], axis=1
        )

    gradient = whole(0, cut, rows)
    col_state = whole(piece, at + 2 * all_rows + gap, 1)[0]
    row_total = totals[0] / all_rows
    entries = float(all_rows * COLS)
    update_rms = jnp.sqrt(row_total * totals[1] / entries)
    update_rms = lax.optimization_barrier(update_rms)
    param_rms = jnp.sqrt(totals[2] / entries + 1e-06)
    scale = 0.01 * param_rms * jnp.sqrt(row_total) / jnp.maximum(1.0, update_rms)
    update = gradient / jnp.sqrt(row_state[:, None] * col_state[None, :])
    updated = param - scale[:, None] * update
    return (updated, row_state, col_state, update_rms[0])


def solution(mesh):
    in_specs = (P("dp", "mp", None), P("mp", "dp"), P("mp"), P("dp"))
    out_specs = (P("mp", "dp"), P("mp"), P("dp"), P())
    return jax.shard_map(
        on_device, mesh=mesh, in_specs=in_specs, out_specs=out_specs, check_vma=False
    )
```

```python
import jax
import jax.numpy as jnp
from jax import lax
from jax.sharding import PartitionSpec as P

COLS = 73728
LANES = 128


def everyone(value, axis, size):
    sent = jnp.broadcast_to(value[None], (size, *value.shape))
    return lax.all_to_all(sent, axis, 0, 0, tiled=True)


def on_device(grad_parts, param, row_prior, col_prior):
    replicas = lax.axis_size("dp")
    slabs = lax.axis_size("mp")
    rows = grad_parts.shape[1]
    own = param.shape[1]
    all_rows = rows * slabs
    pairs = replicas // 2
    core = lax.axis_index("dp") % 2
    far, near, wide = replicas // 8, 4, 2
    deep = slabs // wide
    half = own // wide
    tiles = deep * LANES
    rest = (half - tiles) // deep
    slab = lax.axis_index("mp")
    across, along = slab // deep, slab % deep

    def device(f, n, c, x, y):
        return (deep * x + y) * replicas + 8 * f + 2 * n + c

    blocks = grad_parts[0].reshape(rows, pairs, 2, own).transpose(2, 1, 0, 3)
    sent = lax.dynamic_index_in_dim(blocks, 1 - core, 0, keepdims=False).astype(jnp.float32)
    kept = lax.dynamic_index_in_dim(blocks, core, 0, keepdims=False)
    got = lax.ppermute(sent, "dp", [(i, i ^ 1) for i in range(replicas)])
    place = wide * along + across
    lines = jnp.arange(rows)[:, None] + place * rows
    own_lane = jnp.where(jnp.arange(all_rows)[None, :] == lines, 1.0, 0.0)
    old_part = lax.optimization_barrier(0.9 * col_prior)
    tile_at = half * across + LANES * along
    rest_at = half * across + tiles + rest * along
    tile_old = lax.dynamic_slice(old_part, (tile_at.astype(jnp.uint32),), (LANES,))
    rest_old = lax.dynamic_slice(old_part, (rest_at.astype(jnp.uint32),), (rest,))
    own_slab = jnp.arange(slabs)[:, None] == place
    old_rows = jnp.where(own_slab, (0.9 * row_prior / replicas)[None, :], 0.0)
    param_part = jnp.sum(param * param, axis=1)
    got, param_part, old_rows, tile_old, rest_old, own_lane = lax.optimization_barrier(
        (got, param_part, old_rows, tile_old, rest_old, own_lane)
    )
    both = kept.astype(jnp.float32) + got

    both = both.reshape(far, near, rows, own)
    both = jnp.concatenate(
        [both[:, n, :, half * x : half * (x + 1)] for n in range(near) for x in range(wide)]
    ).reshape(near * wide, far, rows, half)
    near_groups = [
        [device(f, n, c, x, y) for n in range(near) for x in range(wide)]
        for f in range(far)
        for c in range(2)
        for y in range(deep)
    ]
    parts = lax.all_to_all(both, ("mp", "dp"), 0, 0, tiled=True, axis_index_groups=near_groups)
    parts = jnp.sum(parts.reshape(near, wide, far, rows, half), axis=0)

    main = parts[..., :tiles].reshape(wide, far, rows, deep, LANES).transpose(1, 3, 0, 2, 4)
    side = parts[..., tiles:].reshape(wide, far, rows, deep, rest).transpose(1, 3, 0, 2, 4)
    cut = rows * LANES
    piece = cut + rows * rest
    sent = jnp.concatenate(
        [
            main.reshape(far * deep, 1, wide * cut),
            side.reshape(far * deep, 1, wide * rows * rest),
        ],
        axis=2,
    )
    far_groups = [
        [device(f, n, c, x, y) for f in range(far) for y in range(deep)]
        for n in range(near)
        for c in range(2)
        for x in range(wide)
    ]
    parts = lax.all_to_all(sent, ("mp", "dp"), 0, 0, tiled=True, axis_index_groups=far_groups)
    gradient = jnp.sum(parts.reshape(far, deep, 1, wide * piece), axis=0) / replicas

    flat = gradient[:, 0]
    halves = (
        flat[:, : wide * cut].reshape(slabs, rows, LANES),
        flat[:, wide * cut :].reshape(slabs, rows, rest),
    )
    power = [value * value for value in halves]
    squares = [value + 1e-30 for value in power]
    cols = [
        old + 0.1 * jnp.sum(value, axis=(0, 1)) / all_rows
        for old, value in zip((tile_old, rest_old), squares)
    ]

    def along_rows(tile_value, rest_value):
        gap = LANES - rest
        return jnp.sum(tile_value + jnp.pad(rest_value, ((0, 0), (0, 0), (0, gap))), axis=2)

    row_part = old_rows + 0.1 * along_rows(*squares) / COLS
    scaled_part = along_rows(*(value / c for value, c in zip(power, cols)))
    sums = jnp.concatenate(
        [
            jnp.stack([row_part, scaled_part]).reshape(2 * all_rows),
            jnp.pad(param_part, (0, all_rows - rows)),
        ]
    )[None]
    gap = 2 * rows
    rest_cols = jnp.pad(cols[1], (2 * all_rows + gap, all_rows - gap - rest))[None]
    known = jnp.broadcast_to(cols[0], (slabs, 1, LANES))
    main = gradient[:, 0, : wide * cut].reshape(deep, wide, cut).transpose(1, 0, 2)
    side = gradient[:, 0, wide * cut :].reshape(deep, wide, piece - cut).transpose(1, 0, 2)
    known = jnp.concatenate(
        [main.reshape(slabs, 1, cut), side.reshape(slabs, 1, piece - cut), known], axis=2
    )
    sums, known, rest_cols = lax.optimization_barrier((sums, known, rest_cols))
    sums = jnp.sum(everyone(sums, "dp", replicas), axis=0) + rest_cols

    known = jnp.concatenate([known, jnp.broadcast_to(sums, (slabs, *sums.shape))], axis=2)
    known = lax.all_to_all(known, "mp", 0, 0, tiled=True)
    at = piece + LANES
    sums = jnp.sum(known[:, 0, at:], axis=0)
    row_states, scaled_sum, param_sum = (sums[i * all_rows : (i + 1) * all_rows] for i in range(3))
    param_sum = jnp.where(jnp.arange(all_rows) < rows, param_sum, 0.0)
    totals = jnp.stack([row_states, scaled_sum / row_states, param_sum])
    totals = lax.optimization_barrier(jnp.broadcast_to(totals[:, None, :], (3, rows, all_rows)))
    row_state = jnp.sum(jnp.where(own_lane > 0.0, totals[0], 0.0), axis=1)
    totals = jnp.sum(totals, axis=2)

    def in_columns(start, width, lines):
        value = known[:, 0, start : start + lines * width].reshape(slabs, lines, width)
        value = value.transpose(1, 0, 2).reshape(lines, wide, deep * width)
        return [value[:, x] for x in range(wide)]

    def whole(tile_start, rest_start, lines):
        tile_value = in_columns(tile_start, LANES, lines)
        rest_value = in_columns(rest_start, rest, lines)
        return jnp.concatenate(
            [v for pair in zip(tile_value, rest_value) for v in pair], axis=1
        )

    gradient = whole(0, cut, rows)
    col_state = whole(piece, at + 2 * all_rows + gap, 1)[0]
    row_total = totals[0] / all_rows
    entries = float(all_rows * COLS)
    update_rms = jnp.sqrt(row_total * totals[1] / entries)
    update_rms = lax.optimization_barrier(update_rms)
    param_rms = jnp.sqrt(totals[2] / entries + 1e-06)
    scale = 0.01 * param_rms * jnp.sqrt(row_total) / jnp.maximum(1.0, update_rms)
    update = gradient / jnp.sqrt(row_state[:, None] * col_state[None, :])
    updated = param - scale[:, None] * update
    return (updated, row_state, col_state, update_rms[0])


def solution(mesh):
    in_specs = (P("dp", "mp", None), P("mp", "dp"), P("mp"), P("dp"))
    out_specs = (P("mp", "dp"), P("mp"), P("dp"), P())
    return jax.shard_map(
        on_device, mesh=mesh, in_specs=in_specs, out_specs=out_specs, check_vma=False
    )
```
